512 devices in a mesh: pair: 32 (over z_lo, y, core), va: 4 (over z_hi), vb: 4 (over x).
Axes of the slice: x: 4, y: 8, z: 8 (z_hi: 4, z_lo: 2; z = z_hi * 2 + z_lo), core: 2. Of those that a mesh axis runs over, the one named last changes fastest.
Arguments:
- driver: float32 [1600, 256, 256], P('pair', 'va', 'vb'), may hold values from -6 to 6
- coupling: float32 [1600, 1600], P('vb'), may hold values from -0.15625 to 0.15625
- eps_occ: float32 [40], replicated, may hold values from -2 to -0.5
- eps_vir: float32 [256], replicated, may hold values from 0.3 to 3
Outputs:
- spin_adapted: float32 [1600, 256, 256], P('vb', ('va', 'pair'))
The draws below stay inside these ranges and needn't reach their ends.
All inputs are finite; a program needn't handle non-finite values.
Results may differ from the reference program's by a relative error of at most 0.0001.
Values sent between devices are 32-bit elements; how exact they have to be, the bound alone decides.
A program may use at most 64 MiB of HBM per device.

```python
import jax
import jax.numpy as jnp
from jax import lax

NOCC = 40
V = 256
ITERS = 2
PAIRS = 1600


def levels(rng, shape, pieces, smallest, largest):
    def one(position, shards_of):
        steps = jax.random.uniform(jax.random.fold_in(jax.random.fold_in(rng, 6), position), (shards_of,), jnp.float32, smallest / len(pieces), largest / len(pieces))
        return jnp.repeat(jnp.exp(steps), shape[position] // shards_of).reshape((-1,) + (1,) * (len(shape) - position - 1))

    factor_of = one(*pieces[0])
    for cut in pieces[1:]:
        factor_of = factor_of * one(*cut)
    return factor_of


def bell_draw(stream_key, shape, deviation, most, split=(), held_as=jnp.bfloat16):
    drawn = jax.random.normal(stream_key, shape, jnp.float32) * deviation
    if len(split) > 0:
        drawn = levels(stream_key, shape, split, -0.22, 0.18) * drawn
    return jnp.clip(drawn, min=-most, max=most).astype(held_as)


def setup_inputs(seed: int = 0) -> dict:
    streams_of = jax.random.split(jax.random.key(seed), 5)
    driver = bell_draw(streams_of[0], (PAIRS, V, V), 1.0, 6.0, ((0, 32), (1, 4), (2, 4)), jnp.float32)
    coupling = bell_draw(streams_of[1], (PAIRS, PAIRS), PAIRS ** -0.5, 0.15625, ((0, 4),), jnp.float32)
    eps_occ = jnp.clip(jax.random.uniform(streams_of[2], (NOCC,), jnp.float32, -2.0, -0.5), -2.0, -0.5)
    eps_vir = jnp.clip(jax.random.uniform(streams_of[3], (V,), jnp.float32, 0.3, 3.0), 0.3, 3.0)
    return {"driver": driver, "coupling": coupling, "eps_occ": eps_occ, "eps_vir": eps_vir}


def reference(driver, coupling, eps_occ, eps_vir):
    pair_energy = (eps_occ[:, None] + eps_occ[None, :]).reshape(PAIRS)
    denominator = (eps_vir[:, None] + eps_vir[None, :])[None, :, :] - pair_energy[:, None, None]
    amplitudes = driver / denominator
    for step in range(ITERS):
        ladder = jnp.dot(coupling, amplitudes.reshape(PAIRS, V * V), precision=lax.Precision.HIGHEST, preferred_element_type=jnp.float32)
        amplitudes = (ladder.reshape(PAIRS, V, V) + driver) / denominator
    return 2.0 * amplitudes - jnp.transpose(amplitudes, (0, 2, 1))
```

```python
import jax
import jax.numpy as jnp
from jax import lax
from jax.experimental import pallas as pl
from jax.experimental.pallas import tpu as pltpu
from jax.sharding import PartitionSpec as P

MESH = pl.DeviceIdType.MESH
F32 = jnp.float32
BF16 = jnp.bfloat16

PAIRS = 1600
NOCC = 40
BLK = 400
SRC = 50
ZROWS = (16, 8)
ZOFF = (0, 128)
XROWS = (72, 136)
XOFF = (192, 264)
XHALF = (40, 72)


def kernel(
    drv, cpl, eo, evs, evv, out,
    din, snd, rcv, wf, whi, wlo, dcol, rden, rhs, occ, t2, r1, tn, msend, mrecv, up, qs,
    lsem, vsem, wxs, wxr, xs, xr, zs, zr, cs, cr, ds, dr, c1s, c1r, ms, mr, us, ur,
):
    p = lax.axis_index("pair")
    za = lax.axis_index("va")
    x = lax.axis_index("vb")
    h = lax.rem(p, 2)
    k = p // 2
    y = lax.rem(k, 8)
    zl = k // 8
    z = 2 * za + zl

    def at(pp, aa, xx):
        return {"pair": pp, "va": aa, "vb": xx}

    def zdev(step):
        zz = lax.rem(z + step + 8, 8)
        return at(lax.rem(zz, 2) * 16 + y * 2 + h, zz // 2, x)

    def rcopy(src, dst, s, r, dev):
        return pltpu.make_async_remote_copy(
            src_ref=src, dst_ref=dst, send_sem=s, recv_sem=r, device_id=dev, device_id_type=MESH
        )

    other = at(p + 1 - 2 * h, za, x)

    wcopy = pltpu.make_async_copy(cpl, wf.at[0], lsem.at[0])
    wcopy.start()
    dcopy = pltpu.make_async_copy(drv, din, lsem.at[1])
    dcopy.start()

    bar = pltpu.get_barrier_semaphore()

    @pl.loop(1, 32)
    def _(i):
        pl.semaphore_signal(bar, inc=1, device_id=at(lax.rem(p + i, 32), za, x), device_id_type=MESH)

    for i in range(1, 4):
        pl.semaphore_signal(bar, inc=1, device_id=at(p, za, lax.rem(x + i, 4)), device_id_type=MESH)
        pl.semaphore_signal(bar, inc=1, device_id=at(p, lax.rem(za + i, 4), x), device_id_type=MESH)
    pl.semaphore_signal(bar, inc=1, device_id=zdev(2 * zl - 1), device_id_type=MESH)

    for j in range(NOCC):
        occ[pl.ds(j, 1), :] = jnp.full((1, 128), eo[j], F32)
    lane = lax.broadcasted_iota(jnp.int32, (8, 128), 1)
    cols = jnp.broadcast_to(jnp.where(x >= 2, evv[1:2, :], evv[0:1, :]), (8, 128))
    off = 64 * lax.rem(x, 2) + 32 * h
    cols = pltpu.roll(cols, lax.rem(128 - off, 128), 1)
    vsum = jnp.zeros((8, 128), F32)
    for a in range(4):
        here = (cols if a == 0 else pltpu.roll(cols, 32 * a, 1)) + evs[64 * za + 4 * k + a]
        vsum = jnp.where(lane // 32 == a, here, vsum)
    vrow = vsum[0:1, :]

    @pl.loop(0, NOCC)
    def _(i):
        den = vrow - (occ[...] + eo[i])
        rden[pl.ds(pl.multiple_of(40 * i, 8), 40), :] = 1.0 / den

    wcopy.wait()
    dcopy.wait()
    pl.semaphore_wait(bar, 38)
    for i in range(1, 4):
        pl.semaphore_signal(vsem, inc=1, device_id=at(p, lax.rem(za + i, 4), x), device_id_type=MESH)

    def zslice(hh, zz):
        return pl.ds(pl.multiple_of(ZOFF[hh] + ZROWS[hh] * zz, 8), ZROWS[hh])

    def xslice(hh, half):
        if half is None:
            return pl.ds(XOFF[hh], XROWS[hh])
        return pl.ds(XOFF[hh], XHALF[hh]) if half == 0 else pl.ds(XOFF[hh] + XHALF[hh], XROWS[hh] - XHALF[hh])

    def wx(hh, i):
        return rcopy(
            wf.at[0, zslice(hh, z), :], wf.at[4 - i, zslice(hh, z), :], wxs.at[i - 1], wxr.at[3 - i],
            at(p, za, lax.rem(x + i, 4)),
        )

    def xcopy(hh, n):
        right, left = at(p, za, lax.rem(x + 1, 4)), at(p, za, lax.rem(x + 3, 4))
        if n == 0:
            src, dst, dev = wf.at[0, xslice(hh, None), :], wf.at[3, xslice(hh, None), :], right
        elif n == 1:
            src, dst, dev = wf.at[0, xslice(hh, None), :], wf.at[1, xslice(hh, None), :], left
        elif n == 2:
            src, dst, dev = wf.at[3, xslice(hh, 0), :], wf.at[2, xslice(hh, 0), :], right
        else:
            src, dst, dev = wf.at[1, xslice(hh, 1), :], wf.at[2, xslice(hh, 1), :], left
        return rcopy(src, dst, xs.at[n], xr.at[n], dev)

    def xswap(hh, n):
        rel, half = ((3, None), (1, None), (2, 0), (2, 1))[n]
        ref = wf.at[rel, xslice(hh, half), :]
        return rcopy(ref, ref, cs.at[8 + n], cr.at[8 + n], other)

    def zcopy(hh, up, d):
        src = wf.at[pl.ds(1, 3), zslice(hh, lax.rem(z + 8 + (-d if up else d), 8)), :]
        n = d if up else 4 + d
        return rcopy(src, src, zs.at[n], zr.at[n], zdev(1 if up else -1))

    def zwait(hh, up, d):
        dst = wf.at[pl.ds(1, 3), zslice(hh, lax.rem(z + 8 + (-d if up else d), 8)), :]
        n = d - 1 if up else 4 + d - 1
        return rcopy(dst, dst, zs.at[n], zr.at[n], zdev(1 if up else -1))

    def zswap(hh, dz):
        ref = wf.at[pl.ds(1, 3), zslice(hh, lax.rem(z + dz, 8)), :]
        return rcopy(ref, ref, cs.at[dz], cr.at[dz], other)

    ups, downs = (4, 3), (3, 4)

    for hh in range(2):
        @pl.when(h == hh)
        def _():
            for i in (2, 1, 3):
                wx(hh, i).start()
            for n in range(2):
                xcopy(hh, n).start()

    def dcp(i, d, src):
        return rcopy(snd.at[d], rcv.at[src], ds.at[i], dr.at[src], at(d, za, x))

    @pl.loop(0, 16)
    def _(i):
        kk = lax.rem(k + i, 16)
        rows = [din[pl.ds(4 * kk + a, SRC, stride=64), :] for a in range(4)]
        for hh in range(2):
            d = 2 * kk + hh
            snd[d] = jnp.concatenate([r[:, 32 * hh : 32 * hh + 32] for r in rows], axis=1)

            @pl.when(d != p)
            def _():
                dcp(2 * i + hh, d, p).start()

    def conv(rel):
        @pl.loop(0, 5)
        def _(i):
            rows = pl.ds(pl.multiple_of(80 * i, 16), 80)
            v = wf[rel, rows, :]
            hi = v.astype(BF16)
            whi[rel, rows, :] = hi
            wlo[rel, rows, :] = (v - hi.astype(F32)).astype(BF16)

    def ring(d):
        for hh in range(2):
            @pl.when(h == hh)
            def _():
                if d == 0:
                    for i in range(1, 4):
                        wx(hh, i).wait_recv()
                    zcopy(hh, True, 0).start()
                    zcopy(hh, False, 0).start()
                    zswap(hh, 0).start()
                else:
                    if d <= ups[hh]:
                        zwait(hh, True, d).wait_recv()
                        if d < ups[hh]:
                            zcopy(hh, True, d).start()
                        zswap(hh, 8 - d).start()
                    if d <= downs[hh]:
                        zwait(hh, False, d).wait_recv()
                        if d < downs[hh]:
                            zcopy(hh, False, d).start()
                        zswap(hh, d).start()

    ring(0)
    conv(0)
    ring(1)
    ring(2)
    for hh in range(2):
        @pl.when(h == hh)
        def _():
            for n in range(2):
                xcopy(hh, n).wait_recv()
                xcopy(hh, n + 2).start()
                xswap(hh, n).start()
    ring(3)

    for s in range(32):
        @pl.when(p != s)
        def _():
            dcp(0, 0, s).wait_recv()
            dcol[pl.ds(SRC * s, SRC), :] = rcv[s]

        @pl.when(p == s)
        def _():
            dcol[pl.ds(SRC * s, SRC), :] = snd[s]

    def split(rows, t, slot):
        hi = t.astype(BF16)
        rhs[slot, rows, 0:128] = hi
        rhs[slot, rows, 128:256] = (t - hi.astype(F32)).astype(BF16)

    @pl.loop(0, 4)
    def _(i):
        rows = pl.ds(pl.multiple_of(BLK * i, 16), BLK)
        split(rows, dcol[rows, :] * rden[rows, :], 0)

    ring(4)
    for hh in range(2):
        @pl.when(h == hh)
        def _():
            for n in range(2, 4):
                xcopy(hh, n).wait_recv()
                xswap(hh, n).start()
            for dz in range(8):
                zswap(1 - hh, dz).wait_recv()
            for n in range(4):
                xswap(1 - hh, n).wait_recv()
    for rel in range(1, 4):
        conv(rel)

    def block(rel, slot):
        prod = jnp.dot(whi[rel], rhs[slot], preferred_element_type=F32)
        prod = prod[:, 0:128] + prod[:, 128:256]
        prod = prod + jnp.dot(wlo[rel], rhs[slot, :, 0:128], preferred_element_type=F32)
        rows = pl.ds(pl.multiple_of(BLK * lax.rem(x + rel, 4), 16), BLK)
        return rows, (prod + dcol[rows, :]) * rden[rows, :]

    @pl.loop(0, 4)
    def _(rel):
        rows, t = block(rel, 0)
        split(rows, t, 1)

    def c1(n):
        return rcopy(t2.at[n], r1.at[n], c1s.at[n], c1r.at[n], at(p, za, lax.rem(x + 8 - za - n, 4)))

    def c1_own(n):
        return pltpu.make_async_copy(t2.at[n], r1.at[n], c1r.at[n])

    @pl.loop(0, 4)
    def _(n):
        rel = lax.rem(8 - za - n, 4)
        _rows, t = block(rel, 1)
        t2[n] = t

        @pl.when(rel != 0)
        def _():
            c1(n).start()

        @pl.when(rel == 0)
        def _():
            c1_own(n).start()

    pl.semaphore_wait(vsem, 3)

    def mcp(n, j, zb):
        return rcopy(
            msend.at[n * 16 + j], mrecv.at[za * 16 + k], ms.at[n * 16 + j], mr.at[za * 16 + k],
            at(h * 16 + j, zb, x),
        )

    def ucp(n):
        return rcopy(
            tn.at[n, :, pl.ds(pl.multiple_of(64 * (1 - h), 8), 64), :], up.at[n, h],
            us.at[n], ur.at[n], other,
        )

    lane16 = lax.broadcasted_iota(jnp.int32, (16, 128), 1)

    @pl.loop(0, 4)
    def _(n):
        rel = lax.rem(8 - za - n, 4)

        @pl.when(rel != 0)
        def _():
            c1(n).wait_recv()

        @pl.when(rel == 0)
        def _():
            c1_own(n).wait()

        zb = lax.rem(x + za + n, 4)
        for q in range(4):
            if q < 3:
                v = r1[n, pl.ds(128 * q, 128), :]
            else:
                v = jnp.concatenate([r1[n, pl.ds(384, 16), :], jnp.zeros((112, 128), F32)], axis=0)
            tn[n, q] = v.T
        up[n, h] = tn[n, :, pl.ds(pl.multiple_of(64 * h, 8), 64), :]
        ucp(n).start()
        for q in range(3):
            for b in range(2):
                for a in range(4):
                    qs[q, pl.ds(b * 4 + a, 16, stride=8), :] = tn[n, q, pl.ds(a * 32 + b, 16, stride=2), :]
        rest = jnp.zeros((16, 128), F32)
        for b in range(2):
            for a in range(4):
                g = b * 4 + a
                v = tn[n, 3, pl.ds(a * 32 + b, 16, stride=2), :]
                rest = jnp.where(lane16 // 16 == g, v if g == 0 else pltpu.roll(v, 16 * g, 1), rest)
        for j in range(16):
            m = n * 16 + j
            for q in range(3):
                msend[m, 8 * q : 8 * q + 8, :] = qs[q, 8 * j : 8 * j + 8, :]
            msend[m, 24:25, :] = rest[j : j + 1, :]

        @pl.loop(0, 16)
        def _(i):
            j = lax.rem(k + i, 16)
            own = jnp.logical_and(zb == za, h * 16 + j == p)

            @pl.when(jnp.logical_not(own))
            def _():
                mcp(n, j, zb).start()

            @pl.when(own)
            def _():
                mrecv[za * 16 + k] = msend[n * 16 + j]

    @pl.loop(0, 4)
    def _(n):
        ucp(n).wait_recv()

    @pl.loop(0, 64)
    def _(i):
        own = jnp.logical_and(i // 16 == za, 2 * lax.rem(i, 16) + zl == p)

        @pl.when(jnp.logical_not(own))
        def _():
            rcopy(msend.at[0], mrecv.at[i], ms.at[0], mr.at[i], at(p, za, x)).wait_recv()

    sub = lax.broadcasted_iota(jnp.int32, (16, 8, 128), 1) < 4
    for lt in range(2):
        for q in range(4):
            if q < 3:
                v = mrecv[pl.ds(32 * lt, 32), 8 * q : 8 * q + 8, :].reshape(16, 2, 8, 128)
                even, odd = v[:, 0], v[:, 1]
                mirror = (
                    jnp.where(sub, even, pltpu.roll(odd, 4, 1)).reshape(128, 128),
                    jnp.where(sub, pltpu.roll(even, 4, 1), odd).reshape(128, 128),
                )
            else:
                v = mrecv[pl.ds(32 * lt, 32), 24, :]
                for b in range(2):
                    for a in range(4):
                        g = b * 4 + a
                        qs[b, pl.ds(a, 32, stride=4), :] = v if g == 0 else pltpu.roll(v, 128 - 16 * g, 1)
                mirror = (qs[0], qs[1])
            for b in range(2):
                parts = []
                for s in range(4):
                    xs_ = 2 * lt + s // 2
                    n = lax.rem(xs_ + 8 - x - za, 4)
                    parts.append(up[n, s % 2, q, pl.ds(32 * b, 32), :])
                v = (2.0 * jnp.concatenate(parts, axis=0) - mirror[b]).T
                if q < 3:
                    out[pl.ds(512 * q + 2 * lt + b, 128, stride=4), :] = v
                else:
                    out[pl.ds(1536 + 2 * lt + b, 16, stride=4), :] = v[0:16, :]

    for hh in range(2):
        @pl.when(h == hh)
        def _():
            for i in range(1, 4):
                wx(hh, i).wait_send()
            for n in range(4):
                xcopy(hh, n).wait_send()
                xswap(hh, n).wait_send()
            for d in range(ups[hh]):
                zcopy(hh, True, d).wait_send()
            for d in range(downs[hh]):
                zcopy(hh, False, d).wait_send()
            for dz in range(8):
                zswap(hh, dz).wait_send()

    @pl.loop(0, 32)
    def _(i):
        d = 2 * lax.rem(k + i // 2, 16) + lax.rem(i, 2)

        @pl.when(d != p)
        def _():
            dcp(i, d, p).wait_send()

    @pl.loop(0, 4)
    def _(n):
        @pl.when(lax.rem(8 - za - n, 4) != 0)
        def _():
            c1(n).wait_send()

        ucp(n).wait_send()
        zb = lax.rem(x + za + n, 4)

        @pl.loop(0, 16)
        def _(j):
            @pl.when(jnp.logical_not(jnp.logical_and(zb == za, h * 16 + j == p)))
            def _():
                mcp(n, j, zb).wait_send()


def on_device(driver, coupling, eps_occ, eps_vir):
    dma = pltpu.SemaphoreType.DMA
    any_ = pl.BlockSpec(memory_space=pl.ANY)
    smem = pl.BlockSpec(memory_space=pltpu.SMEM)
    vmem = pl.BlockSpec(memory_space=pltpu.VMEM)
    res = pl.pallas_call(
        kernel,
        out_shape=jax.ShapeDtypeStruct((PAIRS, 128), F32),
        in_specs=[any_, any_, smem, smem, vmem],
        out_specs=vmem,
        scratch_shapes=[
            pltpu.VMEM((3200, 64), F32),
            pltpu.VMEM((32, SRC, 128), F32),
            pltpu.VMEM((32, SRC, 128), F32),
            pltpu.VMEM((4, BLK, PAIRS), F32),
            pltpu.VMEM((4, BLK, PAIRS), BF16),
            pltpu.VMEM((4, BLK, PAIRS), BF16),
            pltpu.VMEM((PAIRS, 128), F32),
            pltpu.VMEM((PAIRS, 128), F32),
            pltpu.VMEM((2, PAIRS, 256), BF16),
            pltpu.VMEM((NOCC, 128), F32),
            pltpu.VMEM((4, BLK, 128), F32),
            pltpu.VMEM((4, BLK, 128), F32),
            pltpu.VMEM((4, 4, 128, 128), F32),
            pltpu.VMEM((64, 25, 128), F32),
            pltpu.VMEM((64, 25, 128), F32),
            pltpu.VMEM((4, 2, 4, 64, 128), F32),
            pltpu.VMEM((3, 128, 128), F32),
            dma((2,)),
            pltpu.SemaphoreType.REGULAR,
            dma((3,)), dma((3,)),
            dma((4,)), dma((4,)),
            dma((8,)), dma((8,)),
            dma((12,)), dma((12,)),
            dma((32,)), dma((32,)),
            dma((4,)), dma((4,)),
            dma((64,)), dma((64,)),
            dma((4,)), dma((4,)),
        ],
        compiler_params=pltpu.CompilerParams(
            collective_id=0, has_side_effects=True, vmem_limit_bytes=56 << 20
        ),
    )(driver.reshape(3200, 64), coupling, eps_occ, eps_vir, eps_vir.reshape(2, 128))
    return res.reshape(BLK, 2, 2, 128).transpose(0, 2, 1, 3).reshape(BLK, 2, 256)


def solution(mesh):
    return jax.shard_map(
        on_device,
        mesh=mesh,
        in_specs=(P("pair", "va", "vb"), P("vb", None), P(), P()),
        out_specs=P("vb", ("va", "pair"), None),
        check_vma=False,
    )
```

```python
import jax
import jax.numpy as jnp
from jax import lax
from jax.experimental import pallas as pl
from jax.experimental.pallas import tpu as pltpu
from jax.sharding import PartitionSpec as P

MESH = pl.DeviceIdType.MESH
F32 = jnp.float32
BF16 = jnp.bfloat16

PAIRS = 1600
NOCC = 40
BLK = 400
SRC = 50
ZROWS = (16, 8)
ZOFF = (0, 128)
XROWS = (72, 136)
XOFF = (192, 264)
XHALF = (40, 72)


def kernel(
    drv, cpl, eo, evs, evv, out,
    din, snd, rcv, wf, whi, wlo, dcol, rden, rhs, occ, t2, r1, tn, msend, mrecv, up, qs,
    lsem, vsem, wxs, wxr, xs, xr, zs, zr, cs, cr, ds, dr, c1s, c1r, ms, mr, us, ur,
):
    p = lax.axis_index("pair")
    za = lax.axis_index("va")
    x = lax.axis_index("vb")
    h = lax.rem(p, 2)
    k = p // 2
    y = lax.rem(k, 8)
    zl = k // 8
    z = 2 * za + zl

    def at(pp, aa, xx):
        return {"pair": pp, "va": aa, "vb": xx}

    def zdev(step):
        zz = lax.rem(z + step + 8, 8)
        return at(lax.rem(zz, 2) * 16 + y * 2 + h, zz // 2, x)

    def rcopy(src, dst, s, r, dev):
        return pltpu.make_async_remote_copy(
            src_ref=src, dst_ref=dst, send_sem=s, recv_sem=r, device_id=dev, device_id_type=MESH
        )

    other = at(p + 1 - 2 * h, za, x)

    wcopy = pltpu.make_async_copy(cpl, wf.at[0], lsem.at[0])
    wcopy.start()
    dcopy = pltpu.make_async_copy(drv, din, lsem.at[1])
    dcopy.start()

    bar = pltpu.get_barrier_semaphore()

    @pl.loop(1, 32)
    def _(i):
        pl.semaphore_signal(bar, inc=1, device_id=at(lax.rem(p + i, 32), za, x), device_id_type=MESH)

    for i in range(1, 4):
        pl.semaphore_signal(bar, inc=1, device_id=at(p, za, lax.rem(x + i, 4)), device_id_type=MESH)
        pl.semaphore_signal(bar, inc=1, device_id=at(p, lax.rem(za + i, 4), x), device_id_type=MESH)
    pl.semaphore_signal(bar, inc=1, device_id=zdev(2 * zl - 1), device_id_type=MESH)

    for j in range(NOCC):
        occ[pl.ds(j, 1), :] = jnp.full((1, 128), eo[j], F32)
    lane = lax.broadcasted_iota(jnp.int32, (8, 128), 1)
    cols = jnp.broadcast_to(jnp.where(x >= 2, evv[1:2, :], evv[0:1, :]), (8, 128))
    off = 64 * lax.rem(x, 2) + 32 * h
    cols = pltpu.roll(cols, lax.rem(128 - off, 128), 1)
    vsum = jnp.zeros((8, 128), F32)
    for a in range(4):
        here = (cols if a == 0 else pltpu.roll(cols, 32 * a, 1)) + evs[64 * za + 4 * k + a]
        vsum = jnp.where(lane // 32 == a, here, vsum)
    vrow = vsum[0:1, :]

    @pl.loop(0, NOCC)
    def _(i):
        den = vrow - (occ[...] + eo[i])
        rden[pl.ds(pl.multiple_of(40 * i, 8), 40), :] = 1.0 / den

    wcopy.wait()
    dcopy.wait()
    pl.semaphore_wait(bar, 38)
    for i in range(1, 4):
        pl.semaphore_signal(vsem, inc=1, device_id=at(p, lax.rem(za + i, 4), x), device_id_type=MESH)

    def zslice(hh, zz):
        return pl.ds(pl.multiple_of(ZOFF[hh] + ZROWS[hh] * zz, 8), ZROWS[hh])

    def xslice(hh, half):
        return pl.ds(XOFF[hh], XHALF[hh]) if half == 0 else pl.ds(XOFF[hh] + XHALF[hh], XROWS[hh] - XHALF[hh])

    def wx(hh, i):
        return rcopy(
            wf.at[0, zslice(hh, z), :], wf.at[4 - i, zslice(hh, z), :], wxs.at[i - 1], wxr.at[3 - i],
            at(p, za, lax.rem(x + i, 4)),
        )

    XPIECES = ((0, 3, 0, True), (0, 1, 1, False), (0, 3, 1, True), (0, 1, 0, False), (3, 2, 0, True), (1, 2, 1, False))

    def xcopy(hh, n):
        here, there, half, right = XPIECES[n]
        return rcopy(
            wf.at[here, xslice(hh, half), :], wf.at[there, xslice(hh, half), :], xs.at[n], xr.at[n],
            at(p, za, lax.rem(x + (1 if right else 3), 4)),
        )

    def xswap(hh, n):
        _here, there, half, _right = XPIECES[n]
        ref = wf.at[there, xslice(hh, half), :]
        return rcopy(ref, ref, cs.at[24 + n], cr.at[24 + n], other)

    def zpiece(hh, rel, dz):
        return wf.at[rel, zslice(hh, lax.rem(z + 8 + dz, 8)), :]

    def zcopy(hh, rel, up, d):
        src = zpiece(hh, rel, -d if up else d)
        n = 3 * (d if up else 4 + d) + rel - 1
        return rcopy(src, src, zs.at[n], zr.at[n], zdev(1 if up else -1))

    def zwait(hh, rel, up, d):
        dst = zpiece(hh, rel, -d if up else d)
        n = 3 * (d - 1 if up else 4 + d - 1) + rel - 1
        return rcopy(dst, dst, zs.at[n], zr.at[n], zdev(1 if up else -1))

    def zswap(hh, rel, dz):
        ref = zpiece(hh, rel, dz)
        n = 3 * dz + rel - 1
        return rcopy(ref, ref, cs.at[n], cr.at[n], other)

    ups, downs = (4, 3), (3, 4)

    def by_core(f):
        for hh in range(2):
            @pl.when(h == hh)
            def _():
                f(hh)

    @by_core
    def _(hh):
        for i in (2, 1, 3):
            wx(hh, i).start()
        for n in range(4):
            xcopy(hh, n).start()

    def dcp(i, d, src):
        return rcopy(snd.at[d], rcv.at[src], ds.at[i], dr.at[src], at(d, za, x))

    @pl.loop(0, 16)
    def _(i):
        kk = lax.rem(k + i, 16)
        rows = [din[pl.ds(4 * kk + a, SRC, stride=64), :] for a in range(4)]
        for hh in range(2):
            d = 2 * kk + hh
            snd[d] = jnp.concatenate([r[:, 32 * hh : 32 * hh + 32] for r in rows], axis=1)

            @pl.when(d != p)
            def _():
                dcp(2 * i + hh, d, p).start()

    def conv(rel):
        @pl.loop(0, 5)
        def _(i):
            rows = pl.ds(pl.multiple_of(80 * i, 16), 80)
            v = wf[rel, rows, :]
            hi = v.astype(BF16)
            whi[rel, rows, :] = hi
            wlo[rel, rows, :] = (v - hi.astype(F32)).astype(BF16)

    RELS = (1, 3, 2)

    def ring(d):
        @by_core
        def _(hh):
            for rel in RELS:
                if d == 0:
                    wx(hh, 4 - rel).wait_recv()
                    zcopy(hh, rel, True, 0).start()
                    zcopy(hh, rel, False, 0).start()
                    zswap(hh, rel, 0).start()
                    continue
                if d <= ups[hh]:
                    zwait(hh, rel, True, d).wait_recv()
                    if d < ups[hh]:
                        zcopy(hh, rel, True, d).start()
                    zswap(hh, rel, 8 - d).start()
                if d <= downs[hh]:
                    zwait(hh, rel, False, d).wait_recv()
                    if d < downs[hh]:
                        zcopy(hh, rel, False, d).start()
                    zswap(hh, rel, d).start()

    def xstep(first, on):
        @by_core
        def _(hh):
            for n in (first, first + 1):
                xcopy(hh, n).wait_recv()
                if on:
                    xcopy(hh, n + 4).start()
                xswap(hh, n).start()

    ring(0)
    conv(0)
    ring(1)
    xstep(0, True)
    ring(2)
    xstep(2, False)
    ring(3)

    for s in range(32):
        @pl.when(p != s)
        def _():
            dcp(0, 0, s).wait_recv()
            dcol[pl.ds(SRC * s, SRC), :] = rcv[s]

        @pl.when(p == s)
        def _():
            dcol[pl.ds(SRC * s, SRC), :] = snd[s]

    def split(rows, t, slot):
        hi = t.astype(BF16)
        rhs[slot, rows, 0:128] = hi
        rhs[slot, rows, 128:256] = (t - hi.astype(F32)).astype(BF16)

    @pl.loop(0, 4)
    def _(i):
        rows = pl.ds(pl.multiple_of(BLK * i, 16), BLK)
        split(rows, dcol[rows, :] * rden[rows, :], 0)

    def block(rel, slot):
        prod = jnp.dot(whi[rel], rhs[slot], preferred_element_type=F32)
        prod = prod[:, 0:128] + prod[:, 128:256]
        prod = prod + jnp.dot(wlo[rel], rhs[slot, :, 0:128], preferred_element_type=F32)
        rows = pl.ds(pl.multiple_of(BLK * lax.rem(x + rel, 4), 16), BLK)
        return rows, (prod + dcol[rows, :]) * rden[rows, :]

    def first(rel):
        rows, t = block(rel, 0)
        split(rows, t, 1)

    ring(4)
    xstep(4, False)
    first(0)
    for rel in RELS:
        @by_core
        def _(hh):
            for dz in range(8):
                zswap(1 - hh, rel, dz).wait_recv()
            for n in range(6):
                if XPIECES[n][1] == rel:
                    xswap(1 - hh, n).wait_recv()
        conv(rel)
        first(rel)

    def c1(n):
        return rcopy(t2.at[n], r1.at[n], c1s.at[n], c1r.at[n], at(p, za, lax.rem(x + 8 - za - n, 4)))

    def c1_own(n):
        return pltpu.make_async_copy(t2.at[n], r1.at[n], c1r.at[n])

    @pl.loop(0, 4)
    def _(n):
        rel = lax.rem(8 - za - n, 4)
        _rows, t = block(rel, 1)
        t2[n] = t

        @pl.when(rel != 0)
        def _():
            c1(n).start()

        @pl.when(rel == 0)
        def _():
            c1_own(n).start()

    pl.semaphore_wait(vsem, 3)

    def mcp(n, j, zb):
        return rcopy(
            msend.at[n * 16 + j], mrecv.at[za * 16 + k], ms.at[n * 16 + j], mr.at[za * 16 + k],
            at(h * 16 + j, zb, x),
        )

    def ucp(n):
        return rcopy(
            tn.at[n, :, pl.ds(pl.multiple_of(64 * (1 - h), 8), 64), :], up.at[n, h],
            us.at[n], ur.at[n], other,
        )

    lane16 = lax.broadcasted_iota(jnp.int32, (16, 128), 1)

    @pl.loop(0, 4)
    def _(n):
        rel = lax.rem(8 - za - n, 4)

        @pl.when(rel != 0)
        def _():
            c1(n).wait_recv()

        @pl.when(rel == 0)
        def _():
            c1_own(n).wait()

        zb = lax.rem(x + za + n, 4)
        for q in range(4):
            if q < 3:
                v = r1[n, pl.ds(128 * q, 128), :]
            else:
                v = jnp.concatenate([r1[n, pl.ds(384, 16), :], jnp.zeros((112, 128), F32)], axis=0)
            tn[n, q] = v.T
        up[n, h] = tn[n, :, pl.ds(pl.multiple_of(64 * h, 8), 64), :]
        ucp(n).start()
        for q in range(3):
            for b in range(2):
                for a in range(4):
                    qs[q, pl.ds(b * 4 + a, 16, stride=8), :] = tn[n, q, pl.ds(a * 32 + b, 16, stride=2), :]
        rest = jnp.zeros((16, 128), F32)
        for b in range(2):
            for a in range(4):
                g = b * 4 + a
                v = tn[n, 3, pl.ds(a * 32 + b, 16, stride=2), :]
                rest = jnp.where(lane16 // 16 == g, v if g == 0 else pltpu.roll(v, 16 * g, 1), rest)
        for j in range(16):
            m = n * 16 + j
            for q in range(3):
                msend[m, 8 * q : 8 * q + 8, :] = qs[q, 8 * j : 8 * j + 8, :]
            msend[m, 24:25, :] = rest[j : j + 1, :]

        @pl.loop(0, 16)
        def _(i):
            j = lax.rem(k + i, 16)
            own = jnp.logical_and(zb == za, h * 16 + j == p)

            @pl.when(jnp.logical_not(own))
            def _():
                mcp(n, j, zb).start()

            @pl.when(own)
            def _():
                mrecv[za * 16 + k] = msend[n * 16 + j]

    @pl.loop(0, 4)
    def _(n):
        ucp(n).wait_recv()

    sub = lax.broadcasted_iota(jnp.int32, (8, 8, 128), 1) < 4

    @pl.loop(0, 4)
    def _(n):
        zs_ = lax.rem(za + 8 - x - n, 4)

        @pl.loop(0, 16)
        def _(j):
            i = zs_ * 16 + j
            own = jnp.logical_and(zs_ == za, 2 * j + zl == p)

            @pl.when(jnp.logical_not(own))
            def _():
                rcopy(msend.at[0], mrecv.at[i], ms.at[0], mr.at[i], at(p, za, x)).wait_recv()

        m = lax.rem(zs_ + 8 - x - za, 4)
        rows = pl.ds(pl.multiple_of(64 * zs_, 64), 64)
        for q in range(4):
            if q < 3:
                v = mrecv[pl.ds(16 * zs_, 16), 8 * q : 8 * q + 8, :].reshape(8, 2, 8, 128)
                even, odd = v[:, 0], v[:, 1]
                mirror = (
                    jnp.where(sub, even, pltpu.roll(odd, 4, 1)).reshape(64, 128),
                    jnp.where(sub, pltpu.roll(even, 4, 1), odd).reshape(64, 128),
                )
            else:
                v = mrecv[pl.ds(16 * zs_, 16), 24, :]
                for b in range(2):
                    for a in range(4):
                        g = b * 4 + a
                        qs[b, pl.ds(a, 16, stride=4), :] = v if g == 0 else pltpu.roll(v, 128 - 16 * g, 1)
                mirror = (qs[0, 0:64, :], qs[1, 0:64, :])
            for b in range(2):
                mine = jnp.concatenate([up[m, s, q, pl.ds(32 * b, 32), :] for s in range(2)], axis=0)
                out[q, b, rows, :] = 2.0 * mine - mirror[b]

    @by_core
    def _(hh):
        for i in range(1, 4):
            wx(hh, i).wait_send()
        for n in range(6):
            xcopy(hh, n).wait_send()
            xswap(hh, n).wait_send()
        for rel in RELS:
            for d in range(ups[hh]):
                zcopy(hh, rel, True, d).wait_send()
            for d in range(downs[hh]):
                zcopy(hh, rel, False, d).wait_send()
            for dz in range(8):
                zswap(hh, rel, dz).wait_send()

    @pl.loop(0, 32)
    def _(i):
        d = 2 * lax.rem(k + i // 2, 16) + lax.rem(i, 2)

        @pl.when(d != p)
        def _():
            dcp(i, d, p).wait_send()

    @pl.loop(0, 4)
    def _(n):
        @pl.when(lax.rem(8 - za - n, 4) != 0)
        def _():
            c1(n).wait_send()

        ucp(n).wait_send()
        zb = lax.rem(x + za + n, 4)

        @pl.loop(0, 16)
        def _(j):
            @pl.when(jnp.logical_not(jnp.logical_and(zb == za, h * 16 + j == p)))
            def _():
                mcp(n, j, zb).wait_send()


def turn(v, out):
    for lt in range(2):
        for b in range(2):
            out[pl.ds(2 * lt + b, 128, stride=4), :] = v[0, b, 128 * lt : 128 * lt + 128, :].T


def on_device(driver, coupling, eps_occ, eps_vir):
    dma = pltpu.SemaphoreType.DMA
    any_ = pl.BlockSpec(memory_space=pl.ANY)
    smem = pl.BlockSpec(memory_space=pltpu.SMEM)
    vmem = pl.BlockSpec(memory_space=pltpu.VMEM)
    res = pl.pallas_call(
        kernel,
        out_shape=jax.ShapeDtypeStruct((4, 2, 256, 128), F32),
        in_specs=[any_, any_, smem, smem, vmem],
        out_specs=vmem,
        scratch_shapes=[
            pltpu.VMEM((3200, 64), F32),
            pltpu.VMEM((32, SRC, 128), F32),
            pltpu.VMEM((32, SRC, 128), F32),
            pltpu.VMEM((4, BLK, PAIRS), F32),
            pltpu.VMEM((4, BLK, PAIRS), BF16),
            pltpu.VMEM((4, BLK, PAIRS), BF16),
            pltpu.VMEM((PAIRS, 128), F32),
            pltpu.VMEM((PAIRS, 128), F32),
            pltpu.VMEM((2, PAIRS, 256), BF16),
            pltpu.VMEM((NOCC, 128), F32),
            pltpu.VMEM((4, BLK, 128), F32),
            pltpu.VMEM((4, BLK, 128), F32),
            pltpu.VMEM((4, 4, 128, 128), F32),
            pltpu.VMEM((64, 25, 128), F32),
            pltpu.VMEM((64, 25, 128), F32),
            pltpu.VMEM((4, 2, 4, 64, 128), F32),
            pltpu.VMEM((3, 128, 128), F32),
            dma((2,)),
            pltpu.SemaphoreType.REGULAR,
            dma((3,)), dma((3,)),
            dma((6,)), dma((6,)),
            dma((24,)), dma((24,)),
            dma((30,)), dma((30,)),
            dma((32,)), dma((32,)),
            dma((4,)), dma((4,)),
            dma((64,)), dma((64,)),
            dma((4,)), dma((4,)),
        ],
        compiler_params=pltpu.CompilerParams(
            collective_id=0, has_side_effects=True, vmem_limit_bytes=56 << 20
        ),
    )(driver.reshape(3200, 64), coupling, eps_occ, eps_vir, eps_vir.reshape(2, 128))
    res = pl.pallas_call(
        turn,
        grid=(4,),
        out_shape=jax.ShapeDtypeStruct((PAIRS, 128), F32),
        in_specs=[pl.BlockSpec((1, 2, 256, 128), lambda i: (i, 0, 0, 0))],
        out_specs=pl.BlockSpec((512, 128), lambda i: (i, 0)),
    )(res)
    return res.reshape(BLK, 2, 2, 128).transpose(0, 2, 1, 3).reshape(BLK, 2, 256)


def solution(mesh):
    return jax.shard_map(
        on_device,
        mesh=mesh,
        in_specs=(P("pair", "va", "vb"), P("vb", None), P(), P()),
        out_specs=P("vb", ("va", "pair"), None),
        check_vma=False,
    )
```

```python
import jax
import jax.numpy as jnp
from jax import lax
from jax.experimental import pallas as pl
from jax.experimental.pallas import tpu as pltpu
from jax.sharding import PartitionSpec as P

MESH = pl.DeviceIdType.MESH
F32 = jnp.float32
BF16 = jnp.bfloat16

PAIRS = 1600
NOCC = 40
BLK = 400
SRC = 50
ZROWS = (16, 8)
ZOFF = (0, 128)
XROWS = (72, 136)
XOFF = (192, 264)
XHALF = (40, 72)


def kernel(
    drv, cpl, eo, evs, evv, out,
    din, snd, rcv, wf, whi, wlo, dcol, rden, rhs, occ, t2, r1, tn, msend, mrecv, up, qs,
    lsem, vsem, wxs, wxr, xs, xr, zs, zr, cs, cr, ds, dr, c1s, c1r, ms, mr, us, ur,
):
    p = lax.axis_index("pair")
    za = lax.axis_index("va")
    x = lax.axis_index("vb")
    h = lax.rem(p, 2)
    k = p // 2
    y = lax.rem(k, 8)
    zl = k // 8
    z = 2 * za + zl

    def at(pp, aa, xx):
        return {"pair": pp, "va": aa, "vb": xx}

    def zdev(step):
        zz = lax.rem(z + step + 8, 8)
        return at(lax.rem(zz, 2) * 16 + y * 2 + h, zz // 2, x)

    def rcopy(src, dst, s, r, dev):
        return pltpu.make_async_remote_copy(
            src_ref=src, dst_ref=dst, send_sem=s, recv_sem=r, device_id=dev, device_id_type=MESH
        )

    other = at(p + 1 - 2 * h, za, x)

    wcopy = pltpu.make_async_copy(cpl, wf.at[0], lsem.at[0])
    wcopy.start()
    dcopy = pltpu.make_async_copy(drv, din, lsem.at[1])
    dcopy.start()

    bar = pltpu.get_barrier_semaphore()

    @pl.loop(1, 32)
    def _(i):
        pl.semaphore_signal(bar, inc=1, device_id=at(lax.rem(p + i, 32), za, x), device_id_type=MESH)

    for i in range(1, 4):
        pl.semaphore_signal(bar, inc=1, device_id=at(p, za, lax.rem(x + i, 4)), device_id_type=MESH)
        pl.semaphore_signal(bar, inc=1, device_id=at(p, lax.rem(za + i, 4), x), device_id_type=MESH)
    pl.semaphore_signal(bar, inc=1, device_id=zdev(2 * zl - 1), device_id_type=MESH)

    for j in range(NOCC):
        occ[pl.ds(j, 1), :] = jnp.full((1, 128), eo[j], F32)
    lane = lax.broadcasted_iota(jnp.int32, (8, 128), 1)
    cols = jnp.broadcast_to(jnp.where(x >= 2, evv[1:2, :], evv[0:1, :]), (8, 128))
    off = 64 * lax.rem(x, 2) + 32 * h
    cols = pltpu.roll(cols, lax.rem(128 - off, 128), 1)
    vsum = jnp.zeros((8, 128), F32)
    for a in range(4):
        here = (cols if a == 0 else pltpu.roll(cols, 32 * a, 1)) + evs[64 * za + 4 * k + a]
        vsum = jnp.where(lane // 32 == a, here, vsum)
    vrow = vsum[0:1, :]

    @pl.loop(0, NOCC)
    def _(i):
        den = vrow - (occ[...] + eo[i])
        rden[pl.ds(pl.multiple_of(40 * i, 8), 40), :] = 1.0 / den

    wcopy.wait()
    dcopy.wait()
    pl.semaphore_wait(bar, 38)
    for i in range(1, 4):
        pl.semaphore_signal(vsem, inc=1, device_id=at(p, lax.rem(za + i, 4), x), device_id_type=MESH)

    def zslice(hh, zz):
        return pl.ds(pl.multiple_of(ZOFF[hh] + ZROWS[hh] * zz, 8), ZROWS[hh])

    def xslice(hh, half):
        return pl.ds(XOFF[hh], XHALF[hh]) if half == 0 else pl.ds(XOFF[hh] + XHALF[hh], XROWS[hh] - XHALF[hh])

    def wx(hh, i):
        return rcopy(
            wf.at[0, zslice(hh, z), :], wf.at[4 - i, zslice(hh, z), :], wxs.at[i - 1], wxr.at[3 - i],
            at(p, za, lax.rem(x + i, 4)),
        )

    XPIECES = ((0, 3, 0, True), (0, 1, 1, False), (0, 3, 1, True), (0, 1, 0, False), (3, 2, 0, True), (1, 2, 1, False))

    def xcopy(hh, n):
        here, there, half, right = XPIECES[n]
        return rcopy(
            wf.at[here, xslice(hh, half), :], wf.at[there, xslice(hh, half), :], xs.at[n], xr.at[n],
            at(p, za, lax.rem(x + (1 if right else 3), 4)),
        )

    def xswap(hh, n):
        _here, there, half, _right = XPIECES[n]
        ref = wf.at[there, xslice(hh, half), :]
        return rcopy(ref, ref, cs.at[24 + n], cr.at[24 + n], other)

    def zpiece(hh, rel, dz):
        return wf.at[rel, zslice(hh, lax.rem(z + 8 + dz, 8)), :]

    def zcopy(hh, rel, up, d):
        src = zpiece(hh, rel, -d if up else d)
        n = 3 * (d if up else 4 + d) + rel - 1
        return rcopy(src, src, zs.at[n], zr.at[n], zdev(1 if up else -1))

    def zwait(hh, rel, up, d):
        dst = zpiece(hh, rel, -d if up else d)
        n = 3 * (d - 1 if up else 4 + d - 1) + rel - 1
        return rcopy(dst, dst, zs.at[n], zr.at[n], zdev(1 if up else -1))

    def zswap(hh, rel, dz):
        ref = zpiece(hh, rel, dz)
        n = 3 * dz + rel - 1
        return rcopy(ref, ref, cs.at[n], cr.at[n], other)

    ups, downs = (4, 3), (3, 4)

    def by_core(f):
        for hh in range(2):
            @pl.when(h == hh)
            def _():
                f(hh)

    @by_core
    def _(hh):
        for i in (2, 1, 3):
            wx(hh, i).start()
        for n in range(4):
            xcopy(hh, n).start()

    def dcp(i, d, src):
        return rcopy(snd.at[d], rcv.at[src], ds.at[i], dr.at[src], at(d, za, x))

    def dsend(lo, hi):
        @pl.loop(lo, hi)
        def _(i):
            kk = lax.rem(k + i, 16)
            rows = [din[pl.ds(4 * kk + a, SRC, stride=64), :] for a in range(4)]
            for hh in range(2):
                d = 2 * kk + hh
                snd[d] = jnp.concatenate([r[:, 32 * hh : 32 * hh + 32] for r in rows], axis=1)

                @pl.when(d != p)
                def _():
                    dcp(2 * i + hh, d, p).start()

    def conv(rel):
        @pl.loop(0, 5)
        def _(i):
            rows = pl.ds(pl.multiple_of(80 * i, 16), 80)
            v = wf[rel, rows, :]
            hi = v.astype(BF16)
            whi[rel, rows, :] = hi
            wlo[rel, rows, :] = (v - hi.astype(F32)).astype(BF16)

    RELS = (1, 3, 2)

    def ring(d):
        @by_core
        def _(hh):
            for rel in RELS:
                if d == 0:
                    wx(hh, 4 - rel).wait_recv()
                    zcopy(hh, rel, True, 0).start()
                    zcopy(hh, rel, False, 0).start()
                    zswap(hh, rel, 0).start()
                    continue
                if d <= ups[hh]:
                    zwait(hh, rel, True, d).wait_recv()
                    if d < ups[hh]:
                        zcopy(hh, rel, True, d).start()
                    zswap(hh, rel, 8 - d).start()
                if d <= downs[hh]:
                    zwait(hh, rel, False, d).wait_recv()
                    if d < downs[hh]:
                        zcopy(hh, rel, False, d).start()
                    zswap(hh, rel, d).start()

    def xstep(first, on):
        @by_core
        def _(hh):
            for n in (first, first + 1):
                xcopy(hh, n).wait_recv()
                if on:
                    xcopy(hh, n + 4).start()
                xswap(hh, n).start()

    dsend(0, 16)
    ring(0)
    conv(0)
    ring(1)
    xstep(0, True)
    ring(2)
    xstep(2, False)
    ring(3)

    for s in range(32):
        @pl.when(p != s)
        def _():
            dcp(0, 0, s).wait_recv()
            dcol[pl.ds(SRC * s, SRC), :] = rcv[s]

        @pl.when(p == s)
        def _():
            dcol[pl.ds(SRC * s, SRC), :] = snd[s]

    def split(rows, t, slot):
        hi = t.astype(BF16)
        rhs[slot, rows, 0:128] = hi
        rhs[slot, rows, 128:256] = (t - hi.astype(F32)).astype(BF16)

    @pl.loop(0, 4)
    def _(i):
        rows = pl.ds(pl.multiple_of(BLK * i, 16), BLK)
        split(rows, dcol[rows, :] * rden[rows, :], 0)

    def block(rel, slot):
        prod = jnp.dot(whi[rel], rhs[slot], preferred_element_type=F32)
        prod = prod[:, 0:128] + prod[:, 128:256]
        prod = prod + jnp.dot(wlo[rel], rhs[slot, :, 0:128], preferred_element_type=F32)
        rows = pl.ds(pl.multiple_of(BLK * lax.rem(x + rel, 4), 16), BLK)
        return rows, (prod + dcol[rows, :]) * rden[rows, :]

    def first(rel):
        rows, t = block(rel, 0)
        split(rows, t, 1)

    ring(4)
    xstep(4, False)
    first(0)
    for rel in RELS:
        @by_core
        def _(hh):
            for dz in range(8):
                zswap(1 - hh, rel, dz).wait_recv()
            for n in range(6):
                if XPIECES[n][1] == rel:
                    xswap(1 - hh, n).wait_recv()
        conv(rel)
        first(rel)

    sg = 1 - 2 * lax.rem(y, 2)

    def shift(n):
        return lax.rem(sg * (za + n) + 8, 4)

    def c1(n):
        return rcopy(t2.at[n], r1.at[n], c1s.at[n], c1r.at[n], at(p, za, lax.rem(x + 4 - shift(n), 4)))

    def c1_own(n):
        return pltpu.make_async_copy(t2.at[n], r1.at[n], c1r.at[n])

    @pl.loop(0, 4)
    def _(n):
        rel = lax.rem(4 - shift(n), 4)
        _rows, t = block(rel, 1)
        t2[n] = t

        @pl.when(rel != 0)
        def _():
            c1(n).start()

        @pl.when(rel == 0)
        def _():
            c1_own(n).start()

    pl.semaphore_wait(vsem, 3)

    def mcp(n, j, zb):
        return rcopy(
            msend.at[n * 16 + j], mrecv.at[za * 16 + k], ms.at[n * 16 + j], mr.at[za * 16 + k],
            at(h * 16 + j, zb, x),
        )

    def ucp(n):
        return rcopy(
            tn.at[n, :, pl.ds(pl.multiple_of(64 * (1 - h), 8), 64), :], up.at[n, h],
            us.at[n], ur.at[n], other,
        )

    lane16 = lax.broadcasted_iota(jnp.int32, (16, 128), 1)

    @pl.loop(0, 4)
    def _(n):
        rel = lax.rem(4 - shift(n), 4)

        @pl.when(rel != 0)
        def _():
            c1(n).wait_recv()

        @pl.when(rel == 0)
        def _():
            c1_own(n).wait()

        zb = lax.rem(x + shift(n), 4)
        for q in range(4):
            if q < 3:
                v = r1[n, pl.ds(128 * q, 128), :]
            else:
                v = jnp.concatenate([r1[n, pl.ds(384, 16), :], jnp.zeros((112, 128), F32)], axis=0)
            tn[n, q] = v.T
        up[n, h] = tn[n, :, pl.ds(pl.multiple_of(64 * h, 8), 64), :]
        ucp(n).start()
        for q in range(3):
            for b in range(2):
                for a in range(4):
                    qs[q, pl.ds(b * 4 + a, 16, stride=8), :] = tn[n, q, pl.ds(a * 32 + b, 16, stride=2), :]
        rest = jnp.zeros((16, 128), F32)
        for b in range(2):
            for a in range(4):
                g = b * 4 + a
                v = tn[n, 3, pl.ds(a * 32 + b, 16, stride=2), :]
                rest = jnp.where(lane16 // 16 == g, v if g == 0 else pltpu.roll(v, 16 * g, 1), rest)
        for j in range(16):
            m = n * 16 + j
            for q in range(3):
                msend[m, 8 * q : 8 * q + 8, :] = qs[q, 8 * j : 8 * j + 8, :]
            msend[m, 24:25, :] = rest[j : j + 1, :]

        @pl.loop(0, 16)
        def _(i):
            j = lax.rem(k + i, 16)
            own = jnp.logical_and(zb == za, h * 16 + j == p)

            @pl.when(jnp.logical_not(own))
            def _():
                mcp(n, j, zb).start()

            @pl.when(own)
            def _():
                mrecv[za * 16 + k] = msend[n * 16 + j]

    @pl.loop(0, 4)
    def _(n):
        ucp(n).wait_recv()

    sub = lax.broadcasted_iota(jnp.int32, (8, 8, 128), 1) < 4

    @pl.loop(0, 4)
    def _(n):
        zs_ = lax.rem(za + 8 - x - n, 4)

        @pl.loop(0, 16)
        def _(j):
            i = zs_ * 16 + j
            own = jnp.logical_and(zs_ == za, 2 * j + zl == p)

            @pl.when(jnp.logical_not(own))
            def _():
                rcopy(msend.at[0], mrecv.at[i], ms.at[0], mr.at[i], at(p, za, x)).wait_recv()

        m = lax.rem(sg * (zs_ - x) + 12 - za, 4)
        rows = pl.ds(pl.multiple_of(64 * zs_, 64), 64)
        for q in range(4):
            if q < 3:
                v = mrecv[pl.ds(16 * zs_, 16), 8 * q : 8 * q + 8, :].reshape(8, 2, 8, 128)
                even, odd = v[:, 0], v[:, 1]
                mirror = (
                    jnp.where(sub, even, pltpu.roll(odd, 4, 1)).reshape(64, 128),
                    jnp.where(sub, pltpu.roll(even, 4, 1), odd).reshape(64, 128),
                )
            else:
                v = mrecv[pl.ds(16 * zs_, 16), 24, :]
                for b in range(2):
                    for a in range(4):
                        g = b * 4 + a
                        qs[b, pl.ds(a, 16, stride=4), :] = v if g == 0 else pltpu.roll(v, 128 - 16 * g, 1)
                mirror = (qs[0, 0:64, :], qs[1, 0:64, :])
            for b in range(2):
                mine = jnp.concatenate([up[m, s, q, pl.ds(32 * b, 32), :] for s in range(2)], axis=0)
                out[q, b, rows, :] = 2.0 * mine - mirror[b]

    @by_core
    def _(hh):
        for i in range(1, 4):
            wx(hh, i).wait_send()
        for n in range(6):
            xcopy(hh, n).wait_send()
            xswap(hh, n).wait_send()
        for rel in RELS:
            for d in range(ups[hh]):
                zcopy(hh, rel, True, d).wait_send()
            for d in range(downs[hh]):
                zcopy(hh, rel, False, d).wait_send()
            for dz in range(8):
                zswap(hh, rel, dz).wait_send()

    @pl.loop(0, 32)
    def _(i):
        d = 2 * lax.rem(k + i // 2, 16) + lax.rem(i, 2)

        @pl.when(d != p)
        def _():
            dcp(i, d, p).wait_send()

    @pl.loop(0, 4)
    def _(n):
        @pl.when(lax.rem(4 - shift(n), 4) != 0)
        def _():
            c1(n).wait_send()

        ucp(n).wait_send()
        zb = lax.rem(x + shift(n), 4)

        @pl.loop(0, 16)
        def _(j):
            @pl.when(jnp.logical_not(jnp.logical_and(zb == za, h * 16 + j == p)))
            def _():
                mcp(n, j, zb).wait_send()


def turn(v, out):
    for q in range(4):
        n = 128 if q < 3 else 16
        for lt in range(2):
            for b in range(2):
                out[pl.ds(512 * q + 2 * lt + b, n, stride=4), :] = v[q, b, 128 * lt : 128 * lt + 128, :].T[0:n]


def on_device(driver, coupling, eps_occ, eps_vir):
    dma = pltpu.SemaphoreType.DMA
    any_ = pl.BlockSpec(memory_space=pl.ANY)
    smem = pl.BlockSpec(memory_space=pltpu.SMEM)
    vmem = pl.BlockSpec(memory_space=pltpu.VMEM)
    res = pl.pallas_call(
        kernel,
        out_shape=jax.ShapeDtypeStruct((4, 2, 256, 128), F32),
        in_specs=[any_, any_, smem, smem, vmem],
        out_specs=vmem,
        scratch_shapes=[
            pltpu.VMEM((3200, 64), F32),
            pltpu.VMEM((32, SRC, 128), F32),
            pltpu.VMEM((32, SRC, 128), F32),
            pltpu.VMEM((4, BLK, PAIRS), F32),
            pltpu.VMEM((4, BLK, PAIRS), BF16),
            pltpu.VMEM((4, BLK, PAIRS), BF16),
            pltpu.VMEM((PAIRS, 128), F32),
            pltpu.VMEM((PAIRS, 128), F32),
            pltpu.VMEM((2, PAIRS, 256), BF16),
            pltpu.VMEM((NOCC, 128), F32),
            pltpu.VMEM((4, BLK, 128), F32),
            pltpu.VMEM((4, BLK, 128), F32),
            pltpu.VMEM((4, 4, 128, 128), F32),
            pltpu.VMEM((64, 25, 128), F32),
            pltpu.VMEM((64, 25, 128), F32),
            pltpu.VMEM((4, 2, 4, 64, 128), F32),
            pltpu.VMEM((3, 128, 128), F32),
            dma((2,)),
            pltpu.SemaphoreType.REGULAR,
            dma((3,)), dma((3,)),
            dma((6,)), dma((6,)),
            dma((24,)), dma((24,)),
            dma((30,)), dma((30,)),
            dma((32,)), dma((32,)),
            dma((4,)), dma((4,)),
            dma((64,)), dma((64,)),
            dma((4,)), dma((4,)),
        ],
        compiler_params=pltpu.CompilerParams(
            collective_id=0, has_side_effects=True, vmem_limit_bytes=56 << 20
        ),
    )(driver.reshape(3200, 64), coupling, eps_occ, eps_vir, eps_vir.reshape(2, 128))
    res = pl.pallas_call(
        turn,
        out_shape=jax.ShapeDtypeStruct((PAIRS, 128), F32),
        in_specs=[vmem],
        out_specs=vmem,
        compiler_params=pltpu.CompilerParams(vmem_limit_bytes=8 << 20),
    )(res)
    return res.reshape(BLK, 2, 2, 128).transpose(0, 2, 1, 3).reshape(BLK, 2, 256)


def solution(mesh):
    return jax.shard_map(
        on_device,
        mesh=mesh,
        in_specs=(P("pair", "va", "vb"), P("vb", None), P(), P()),
        out_specs=P("vb", ("va", "pair"), None),
        check_vma=False,
    )
```

```python
import jax
import jax.numpy as jnp
from jax import lax
from jax.experimental import pallas as pl
from jax.experimental.pallas import tpu as pltpu
from jax.sharding import PartitionSpec as P

MESH = pl.DeviceIdType.MESH
F32 = jnp.float32
BF16 = jnp.bfloat16

PAIRS = 1600
NOCC = 40
BLK = 400
SRC = 50
ZROWS = (16, 8)
ZOFF = (0, 128)
XROWS = (72, 136)
XOFF = (192, 264)
XHALF = (40, 72)


def kernel(
    drv, cpl, eo, evs, evv, out,
    din, snd, rcv, wf, whi, wlo, dcol, rden, rhs, occ, t2, r1, tn, msend, mrecv, up, qs,
    lsem, vsem, wxs, wxr, xs, xr, zs, zr, cs, cr, ds, dr, c1s, c1r, ms, mr, us, ur,
):
    p = lax.axis_index("pair")
    za = lax.axis_index("va")
    x = lax.axis_index("vb")
    h = lax.rem(p, 2)
    k = p // 2
    y = lax.rem(k, 8)
    zl = k // 8
    z = 2 * za + zl

    def at(pp, aa, xx):
        return {"pair": pp, "va": aa, "vb": xx}

    def zdev(step):
        zz = lax.rem(z + step + 8, 8)
        return at(lax.rem(zz, 2) * 16 + y * 2 + h, zz // 2, x)

    def rcopy(src, dst, s, r, dev):
        return pltpu.make_async_remote_copy(
            src_ref=src, dst_ref=dst, send_sem=s, recv_sem=r, device_id=dev, device_id_type=MESH
        )

    other = at(p + 1 - 2 * h, za, x)

    wcopy = pltpu.make_async_copy(cpl, wf.at[0], lsem.at[0])
    wcopy.start()
    dcopy = pltpu.make_async_copy(drv, din, lsem.at[1])
    dcopy.start()

    bar = pltpu.get_barrier_semaphore()

    @pl.loop(1, 32)
    def _(i):
        pl.semaphore_signal(bar, inc=1, device_id=at(lax.rem(p + i, 32), za, x), device_id_type=MESH)

    for i in range(1, 4):
        pl.semaphore_signal(bar, inc=1, device_id=at(p, za, lax.rem(x + i, 4)), device_id_type=MESH)
        pl.semaphore_signal(bar, inc=1, device_id=at(p, lax.rem(za + i, 4), x), device_id_type=MESH)
    pl.semaphore_signal(bar, inc=1, device_id=zdev(2 * zl - 1), device_id_type=MESH)

    for j in range(NOCC):
        occ[pl.ds(j, 1), :] = jnp.full((1, 128), eo[j], F32)
    lane = lax.broadcasted_iota(jnp.int32, (8, 128), 1)
    cols = jnp.broadcast_to(jnp.where(x >= 2, evv[1:2, :], evv[0:1, :]), (8, 128))
    off = 64 * lax.rem(x, 2) + 32 * h
    cols = pltpu.roll(cols, lax.rem(128 - off, 128), 1)
    vsum = jnp.zeros((8, 128), F32)
    for a in range(4):
        here = (cols if a == 0 else pltpu.roll(cols, 32 * a, 1)) + evs[64 * za + 4 * k + a]
        vsum = jnp.where(lane // 32 == a, here, vsum)
    vrow = vsum[0:1, :]

    @pl.loop(0, NOCC)
    def _(i):
        den = vrow - (occ[...] + eo[i])
        rden[pl.ds(pl.multiple_of(40 * i, 8), 40), :] = 1.0 / den

    wcopy.wait()
    dcopy.wait()
    pl.semaphore_wait(bar, 38)
    for i in range(1, 4):
        pl.semaphore_signal(vsem, inc=1, device_id=at(p, lax.rem(za + i, 4), x), device_id_type=MESH)

    def zslice(hh, zz):
        return pl.ds(pl.multiple_of(ZOFF[hh] + ZROWS[hh] * zz, 8), ZROWS[hh])

    def xslice(hh, half):
        return pl.ds(XOFF[hh], XHALF[hh]) if half == 0 else pl.ds(XOFF[hh] + XHALF[hh], XROWS[hh] - XHALF[hh])

    def wx(hh, i):
        return rcopy(
            wf.at[0, zslice(hh, z), :], wf.at[4 - i, zslice(hh, z), :], wxs.at[i - 1], wxr.at[3 - i],
            at(p, za, lax.rem(x + i, 4)),
        )

    XPIECES = ((0, 3, 0, True), (0, 1, 1, False), (0, 3, 1, True), (0, 1, 0, False), (3, 2, 0, True), (1, 2, 1, False))

    def xcopy(hh, n):
        here, there, half, right = XPIECES[n]
        return rcopy(
            wf.at[here, xslice(hh, half), :], wf.at[there, xslice(hh, half), :], xs.at[n], xr.at[n],
            at(p, za, lax.rem(x + (1 if right else 3), 4)),
        )

    def xswap(hh, n):
        _here, there, half, _right = XPIECES[n]
        ref = wf.at[there, xslice(hh, half), :]
        return rcopy(ref, ref, cs.at[24 + n], cr.at[24 + n], other)

    def zpiece(hh, rel, dz):
        return wf.at[rel, zslice(hh, lax.rem(z + 8 + dz, 8)), :]

    def zcopy(hh, rel, up, d):
        src = zpiece(hh, rel, -d if up else d)
        n = 3 * (d if up else 4 + d) + rel - 1
        return rcopy(src, src, zs.at[n], zr.at[n], zdev(1 if up else -1))

    def zwait(hh, rel, up, d):
        dst = zpiece(hh, rel, -d if up else d)
        n = 3 * (d - 1 if up else 4 + d - 1) + rel - 1
        return rcopy(dst, dst, zs.at[n], zr.at[n], zdev(1 if up else -1))

    def zswap(hh, rel, dz):
        ref = zpiece(hh, rel, dz)
        n = 3 * dz + rel - 1
        return rcopy(ref, ref, cs.at[n], cr.at[n], other)

    ups, downs = (4, 3), (3, 4)

    def by_core(f):
        for hh in range(2):
            @pl.when(h == hh)
            def _():
                f(hh)

    @by_core
    def _(hh):
        for i in (2, 1, 3):
            wx(hh, i).start()
        for n in range(4):
            xcopy(hh, n).start()

    def dcp(i, d, src):
        return rcopy(snd.at[d], rcv.at[src], ds.at[i], dr.at[src], at(d, za, x))

    def dsend(lo, hi):
        @pl.loop(lo, hi)
        def _(i):
            kk = lax.rem(k + i, 16)
            rows = [din[pl.ds(4 * kk + a, SRC, stride=64), :] for a in range(4)]
            for hh in range(2):
                d = 2 * kk + hh
                snd[d] = jnp.concatenate([r[:, 32 * hh : 32 * hh + 32] for r in rows], axis=1)

                @pl.when(d != p)
                def _():
                    dcp(2 * i + hh, d, p).start()

    def conv(rel):
        @pl.loop(0, 5)
        def _(i):
            rows = pl.ds(pl.multiple_of(80 * i, 16), 80)
            v = wf[rel, rows, :]
            hi = v.astype(BF16)
            whi[rel, rows, :] = hi
            wlo[rel, rows, :] = (v - hi.astype(F32)).astype(BF16)

    RELS = (1, 3, 2)

    def ring(d):
        @by_core
        def _(hh):
            for rel in RELS:
                if d == 0:
                    wx(hh, 4 - rel).wait_recv()
                    zcopy(hh, rel, True, 0).start()
                    zcopy(hh, rel, False, 0).start()
                    zswap(hh, rel, 0).start()
                    continue
                if d <= ups[hh]:
                    zwait(hh, rel, True, d).wait_recv()
                    if d < ups[hh]:
                        zcopy(hh, rel, True, d).start()
                    zswap(hh, rel, 8 - d).start()
                if d <= downs[hh]:
                    zwait(hh, rel, False, d).wait_recv()
                    if d < downs[hh]:
                        zcopy(hh, rel, False, d).start()
                    zswap(hh, rel, d).start()

    def xstep(first, on):
        @by_core
        def _(hh):
            for n in (first, first + 1):
                xcopy(hh, n).wait_recv()
                if on:
                    xcopy(hh, n + 4).start()
                xswap(hh, n).start()

    dsend(0, 16)
    ring(0)
    conv(0)
    ring(1)
    xstep(0, True)
    ring(2)
    xstep(2, False)
    ring(3)

    ring(4)
    xstep(4, False)

    for s in range(32):
        @pl.when(p != s)
        def _():
            dcp(0, 0, s).wait_recv()
            dcol[pl.ds(SRC * s, SRC), :] = rcv[s]

        @pl.when(p == s)
        def _():
            dcol[pl.ds(SRC * s, SRC), :] = snd[s]

    def split(rows, t, slot):
        hi = t.astype(BF16)
        rhs[slot, rows, 0:128] = hi
        rhs[slot, rows, 128:256] = (t - hi.astype(F32)).astype(BF16)

    @pl.loop(0, 4)
    def _(i):
        rows = pl.ds(pl.multiple_of(BLK * i, 16), BLK)
        split(rows, dcol[rows, :] * rden[rows, :], 0)

    def block(rel, slot):
        prod = jnp.dot(whi[rel], rhs[slot], preferred_element_type=F32)
        prod = prod[:, 0:128] + prod[:, 128:256]
        prod = prod + jnp.dot(wlo[rel], rhs[slot, :, 0:128], preferred_element_type=F32)
        rows = pl.ds(pl.multiple_of(BLK * lax.rem(x + rel, 4), 16), BLK)
        return rows, (prod + dcol[rows, :]) * rden[rows, :]

    def first(rel):
        rows, t = block(rel, 0)
        split(rows, t, 1)

    first(0)
    for rel in RELS:
        @by_core
        def _(hh):
            for dz in range(8):
                zswap(1 - hh, rel, dz).wait_recv()
            for n in range(6):
                if XPIECES[n][1] == rel:
                    xswap(1 - hh, n).wait_recv()
        conv(rel)
        first(rel)

    sg = 1 - 2 * lax.rem(y, 2)

    def shift(n):
        return lax.rem(sg * (za + n) + 8, 4)

    def c1(n):
        return rcopy(t2.at[n], r1.at[n], c1s.at[n], c1r.at[n], at(p, za, lax.rem(x + 4 - shift(n), 4)))

    def c1_own(n):
        return pltpu.make_async_copy(t2.at[n], r1.at[n], c1r.at[n])

    @pl.loop(0, 4)
    def _(n):
        rel = lax.rem(4 - shift(n), 4)
        _rows, t = block(rel, 1)
        t2[n] = t

        @pl.when(rel != 0)
        def _():
            c1(n).start()

        @pl.when(rel == 0)
        def _():
            c1_own(n).start()

    pl.semaphore_wait(vsem, 3)

    def mcp(n, j, zb):
        return rcopy(
            msend.at[n * 16 + j], mrecv.at[za * 16 + k], ms.at[n * 16 + j], mr.at[za * 16 + k],
            at(h * 16 + j, zb, x),
        )

    def ucp(n):
        return rcopy(
            tn.at[n, :, pl.ds(pl.multiple_of(64 * (1 - h), 8), 64), :], up.at[n, h],
            us.at[n], ur.at[n], other,
        )

    lane16 = lax.broadcasted_iota(jnp.int32, (16, 128), 1)

    @pl.loop(0, 4)
    def _(n):
        rel = lax.rem(4 - shift(n), 4)

        @pl.when(rel != 0)
        def _():
            c1(n).wait_recv()

        @pl.when(rel == 0)
        def _():
            c1_own(n).wait()

        zb = lax.rem(x + shift(n), 4)
        for q in range(4):
            if q < 3:
                v = r1[n, pl.ds(128 * q, 128), :]
            else:
                v = jnp.concatenate([r1[n, pl.ds(384, 16), :], jnp.zeros((112, 128), F32)], axis=0)
            tn[n, q] = v.T
        up[n, h] = tn[n, :, pl.ds(pl.multiple_of(64 * h, 8), 64), :]
        ucp(n).start()
        for q in range(3):
            for b in range(2):
                for a in range(4):
                    qs[q, pl.ds(b * 4 + a, 16, stride=8), :] = tn[n, q, pl.ds(a * 32 + b, 16, stride=2), :]
        rest = jnp.zeros((16, 128), F32)
        for b in range(2):
            for a in range(4):
                g = b * 4 + a
                v = tn[n, 3, pl.ds(a * 32 + b, 16, stride=2), :]
                rest = jnp.where(lane16 // 16 == g, v if g == 0 else pltpu.roll(v, 16 * g, 1), rest)
        for j in range(16):
            m = n * 16 + j
            for q in range(3):
                msend[m, 8 * q : 8 * q + 8, :] = qs[q, 8 * j : 8 * j + 8, :]
            msend[m, 24:25, :] = rest[j : j + 1, :]

        @pl.loop(0, 16)
        def _(i):
            j = lax.rem(k + i, 16)
            own = jnp.logical_and(zb == za, h * 16 + j == p)

            @pl.when(jnp.logical_not(own))
            def _():
                mcp(n, j, zb).start()

            @pl.when(own)
            def _():
                mrecv[za * 16 + k] = msend[n * 16 + j]

    @pl.loop(0, 4)
    def _(n):
        ucp(n).wait_recv()

    sub = lax.broadcasted_iota(jnp.int32, (8, 8, 128), 1) < 4

    @pl.loop(0, 4)
    def _(n):
        zs_ = lax.rem(za + 8 - x - n, 4)

        @pl.loop(0, 16)
        def _(j):
            i = zs_ * 16 + j
            own = jnp.logical_and(zs_ == za, 2 * j + zl == p)

            @pl.when(jnp.logical_not(own))
            def _():
                rcopy(msend.at[0], mrecv.at[i], ms.at[0], mr.at[i], at(p, za, x)).wait_recv()

        m = lax.rem(sg * (zs_ - x) + 12 - za, 4)
        rows = pl.ds(pl.multiple_of(64 * zs_, 64), 64)
        for q in range(4):
            if q < 3:
                v = mrecv[pl.ds(16 * zs_, 16), 8 * q : 8 * q + 8, :].reshape(8, 2, 8, 128)
                even, odd = v[:, 0], v[:, 1]
                mirror = (
                    jnp.where(sub, even, pltpu.roll(odd, 4, 1)).reshape(64, 128),
                    jnp.where(sub, pltpu.roll(even, 4, 1), odd).reshape(64, 128),
                )
            else:
                v = mrecv[pl.ds(16 * zs_, 16), 24, :]
                for b in range(2):
                    for a in range(4):
                        g = b * 4 + a
                        qs[b, pl.ds(a, 16, stride=4), :] = v if g == 0 else pltpu.roll(v, 128 - 16 * g, 1)
                mirror = (qs[0, 0:64, :], qs[1, 0:64, :])
            for b in range(2):
                mine = jnp.concatenate([up[m, s, q, pl.ds(32 * b, 32), :] for s in range(2)], axis=0)
                out[q, b, rows, :] = 2.0 * mine - mirror[b]

    @by_core
    def _(hh):
        for i in range(1, 4):
            wx(hh, i).wait_send()
        for n in range(6):
            xcopy(hh, n).wait_send()
            xswap(hh, n).wait_send()
        for rel in RELS:
            for d in range(ups[hh]):
                zcopy(hh, rel, True, d).wait_send()
            for d in range(downs[hh]):
                zcopy(hh, rel, False, d).wait_send()
            for dz in range(8):
                zswap(hh, rel, dz).wait_send()

    @pl.loop(0, 32)
    def _(i):
        d = 2 * lax.rem(k + i // 2, 16) + lax.rem(i, 2)

        @pl.when(d != p)
        def _():
            dcp(i, d, p).wait_send()

    @pl.loop(0, 4)
    def _(n):
        @pl.when(lax.rem(4 - shift(n), 4) != 0)
        def _():
            c1(n).wait_send()

        ucp(n).wait_send()
        zb = lax.rem(x + shift(n), 4)

        @pl.loop(0, 16)
        def _(j):
            @pl.when(jnp.logical_not(jnp.logical_and(zb == za, h * 16 + j == p)))
            def _():
                mcp(n, j, zb).wait_send()


def turn(v, out):
    for q in range(4):
        n = 128 if q < 3 else 16
        for lt in range(2):
            for b in range(2):
                out[pl.ds(512 * q + 2 * lt + b, n, stride=4), :] = v[q, b, 128 * lt : 128 * lt + 128, :].T[0:n]


def on_device(driver, coupling, eps_occ, eps_vir):
    dma = pltpu.SemaphoreType.DMA
    any_ = pl.BlockSpec(memory_space=pl.ANY)
    smem = pl.BlockSpec(memory_space=pltpu.SMEM)
    vmem = pl.BlockSpec(memory_space=pltpu.VMEM)
    res = pl.pallas_call(
        kernel,
        out_shape=jax.ShapeDtypeStruct((4, 2, 256, 128), F32),
        in_specs=[any_, any_, smem, smem, vmem],
        out_specs=vmem,
        scratch_shapes=[
            pltpu.VMEM((3200, 64), F32),
            pltpu.VMEM((32, SRC, 128), F32),
            pltpu.VMEM((32, SRC, 128), F32),
            pltpu.VMEM((4, BLK, PAIRS), F32),
            pltpu.VMEM((4, BLK, PAIRS), BF16),
            pltpu.VMEM((4, BLK, PAIRS), BF16),
            pltpu.VMEM((PAIRS, 128), F32),
            pltpu.VMEM((PAIRS, 128), F32),
            pltpu.VMEM((2, PAIRS, 256), BF16),
            pltpu.VMEM((NOCC, 128), F32),
            pltpu.VMEM((4, BLK, 128), F32),
            pltpu.VMEM((4, BLK, 128), F32),
            pltpu.VMEM((4, 4, 128, 128), F32),
            pltpu.VMEM((64, 25, 128), F32),
            pltpu.VMEM((64, 25, 128), F32),
            pltpu.VMEM((4, 2, 4, 64, 128), F32),
            pltpu.VMEM((3, 128, 128), F32),
            dma((2,)),
            pltpu.SemaphoreType.REGULAR,
            dma((3,)), dma((3,)),
            dma((6,)), dma((6,)),
            dma((24,)), dma((24,)),
            dma((30,)), dma((30,)),
            dma((32,)), dma((32,)),
            dma((4,)), dma((4,)),
            dma((64,)), dma((64,)),
            dma((4,)), dma((4,)),
        ],
        compiler_params=pltpu.CompilerParams(
            collective_id=0, has_side_effects=True, vmem_limit_bytes=56 << 20
        ),
    )(driver.reshape(3200, 64), coupling, eps_occ, eps_vir, eps_vir.reshape(2, 128))
    res = pl.pallas_call(
        turn,
        out_shape=jax.ShapeDtypeStruct((PAIRS, 128), F32),
        in_specs=[vmem],
        out_specs=vmem,
        compiler_params=pltpu.CompilerParams(vmem_limit_bytes=8 << 20),
    )(res)
    return res.reshape(BLK, 2, 2, 128).transpose(0, 2, 1, 3).reshape(BLK, 2, 256)


def solution(mesh):
    return jax.shard_map(
        on_device,
        mesh=mesh,
        in_specs=(P("pair", "va", "vb"), P("vb", None), P(), P()),
        out_specs=P("vb", ("va", "pair"), None),
        check_vma=False,
    )
```
